256 devices in a mesh: eye: 2 (over core), row: 8 (over z_lo, x), col: 16 (over y, z_hi).
Axes of the slice: x: 4, y: 4, z: 8 (z_hi: 4, z_lo: 2; z = z_hi * 2 + z_lo), core: 2. Of those that a mesh axis runs over, the one named last changes fastest.
Arguments:
- images: bfloat16 [2, 160, 64, 2048], P('eye', 'row', None, 'col'), may hold values from -20 to 20, as said below
- cotangent: bfloat16 [2, 160, 64, 2048], P('eye', 'row', None, 'col'), may hold values from -6 to 6
- conv_weight: bfloat16 [3, 3, 64, 64], replicated, may hold values from -0.25 to 0.25
- query_weight: bfloat16 [64, 64], replicated, may hold values from -0.75 to 0.75
- key_weight: bfloat16 [64, 64], replicated, may hold values from -0.75 to 0.75
- band_start: int32 [2, 8, 16], P('eye', 'row', 'col'), may hold values from 0 to 1536, as said below
- band_width: int32 [2, 8, 16], P('eye', 'row', 'col'), may hold values from 128 to 512, as said below
Outputs:
- refined: bfloat16 [2, 160, 64, 2048], P('eye', 'row', None, 'col')
- input_grad: bfloat16 [2, 160, 64, 2048], P('eye', 'row', None, 'col')
- conv_grad: float32 [3, 3, 64, 64], replicated
- query_grad: float32 [64, 64], replicated
- key_grad: float32 [64, 64], replicated
The draws below stay inside these ranges and needn't reach their ends.
Inputs may be any that keep to these rules, and one draw needn't show every extreme that they name: `images`: the shown draw lies within -4 to 4. `band_start`: A multiple of 128; start + 512 never passes the row's end. `band_width`: A multiple of 128.
All inputs are finite; a program needn't handle non-finite values.
Results may differ from the reference program's by a relative error of at most 0.014.
Values may be sent and summed in bfloat16 or wider, within the bound.
No kernel may reach another device: no remote copies, remote signals or barrier semaphores. Data moves between devices by JAX's collectives and lax.ppermute only.
A program may use at most 128 MiB of HBM per device.

```python
import jax
import jax.numpy as jnp
from jax import lax

CH = 64
TILE_ROWS = 20
TILE_COLS = 128
BAND_PANELS = 4
BAND_COLS = 512
HEIGHT = 160
WIDTH = 2048
N_ROW = 8
N_COL = 16


def draw_images(key, part):
    key = jax.random.fold_in(key, 11)
    shape = (2, HEIGHT, CH, WIDTH)
    values = jnp.clip(jax.random.normal(key, shape, jnp.float32), -4.0, 4.0)
    return values.astype(jnp.bfloat16)


def draw_band_start(key, part):
    key = jax.random.fold_in(key, 21)
    panel = jax.random.randint(key, (2, N_ROW, N_COL), 0, N_COL - BAND_PANELS + 1)
    column = jnp.arange(N_COL, dtype=jnp.int32)[None, None, :]
    panel = jnp.where(column == 0, N_COL - BAND_PANELS, jnp.where(column == 1, 0, panel))
    return (panel * TILE_COLS).astype(jnp.int32)


def draw_band_width(key, part):
    key = jax.random.fold_in(key, 22)
    panels = jax.random.randint(key, (2, N_ROW, N_COL), 1, BAND_PANELS + 1)
    column = jnp.arange(N_COL, dtype=jnp.int32)[None, None, :]
    panels = jnp.where(column == 0, BAND_PANELS, panels)
    return (panels * TILE_COLS).astype(jnp.int32)


def block_levels(stream_key, dims, pieces, least, top_value):
    def one(axis_at, parts):
        heights = jax.random.uniform(jax.random.fold_in(jax.random.fold_in(stream_key, 6), axis_at), (parts,), jnp.float32, least / len(pieces), top_value / len(pieces))
        return jnp.repeat(jnp.exp(heights), dims[axis_at] // parts).reshape((-1,) + (1,) * (len(dims) - axis_at - 1))

    factor_of = one(*pieces[0])
    for cut in pieces[1:]:
        factor_of = factor_of * one(*cut)
    return factor_of


def scatter_about(rng, extent, scale, limit, pieces=(), kind=jnp.bfloat16):
    entries = scale * jax.random.normal(rng, extent, jnp.float32)
    if pieces:
        entries = entries * block_levels(rng, extent, pieces, -0.22, 0.18)
    return jnp.clip(entries, -limit, limit).astype(kind)


def setup_inputs(seed: int = 0) -> dict:
    keys = jax.random.split(jax.random.key(seed), 8)
    return {
        "images": draw_images(jax.random.fold_in(keys[7], 71), 0),
        "cotangent": scatter_about(keys[1], (2, HEIGHT, CH, WIDTH), 1.0, 6.0, ((0, 2), (1, 8), (3, 16))),
        "conv_weight": scatter_about(keys[2], (3, 3, CH, CH), (9 * CH) ** -0.5, 0.25),
        "query_weight": scatter_about(keys[3], (CH, CH), CH ** -0.5, 0.75),
        "key_weight": scatter_about(keys[4], (CH, CH), CH ** -0.5, 0.75),
        "band_start": draw_band_start(jax.random.fold_in(keys[7], 71), 0),
        "band_width": draw_band_width(jax.random.fold_in(keys[7], 71), 0),
    }


def leaky(value):
    return jnp.where(value > 0, value, 0.1 * value)


def slope(value):
    return jnp.where(value > 0, 1.0, 0.1).astype(jnp.float32)


def attend(query_block, grad_block, key_block, value_block, width, scale):
    qf = query_block.astype(jnp.float32)
    gf = grad_block.astype(jnp.float32)
    kf = key_block.astype(jnp.float32)
    vf = value_block.astype(jnp.float32)
    scores = jnp.einsum('hcp,hcj->hpj', qf, kf) * scale
    live = (jnp.arange(key_block.shape[2], dtype=jnp.int32) < width)[None, None, :]
    scores = jnp.where(live, scores, -jnp.inf)
    peak = jnp.max(scores, axis=2, keepdims=True)
    expo = jnp.where(live, jnp.exp(scores - peak), 0.0)
    prob = expo / jnp.sum(expo, axis=2, keepdims=True)
    prob_b = prob.astype(jnp.bfloat16).astype(jnp.float32)
    attended = jnp.einsum('hpj,hcj->hcp', prob_b, vf)
    dprob = jnp.einsum('hcp,hcj->hpj', gf, vf)
    delta = jnp.sum(prob * dprob, axis=2, keepdims=True)
    dscore = (scale * prob * (dprob - delta)).astype(jnp.bfloat16).astype(jnp.float32)
    dquery = jnp.einsum('hpj,hcj->hcp', dscore, kf)
    dkey = jnp.einsum('hpj,hcp->hcj', dscore, qf)
    dvalue = jnp.einsum('hpj,hcp->hcj', prob_b, gf)
    return attended, dquery, dkey, dvalue


def reference(images, cotangent, conv_weight, query_weight, key_weight, band_start, band_width):
    scale = CH ** -0.5
    wconv = conv_weight.astype(jnp.float32)
    wquery = query_weight.astype(jnp.float32)
    wkey = key_weight.astype(jnp.float32)
    height = images.shape[1]
    width_all = images.shape[3]
    padded = jnp.pad(images, ((0, 0), (1, 1), (0, 0), (1, 1))).astype(jnp.float32)
    conv = jnp.zeros(images.shape, jnp.float32)
    for a in range(3):
        for b in range(3):
            conv = conv + jnp.einsum('io,ehiw->ehow', wconv[a, b], padded[:, a:a + height, :, b:b + width_all])
    feat = (images.astype(jnp.float32) + leaky(conv)).astype(jnp.bfloat16)
    featf = feat.astype(jnp.float32)
    query = jnp.einsum('io,ehiw->ehow', wquery, featf).astype(jnp.bfloat16)
    key = jnp.einsum('io,ehiw->ehow', wkey, featf).astype(jnp.bfloat16)
    starts = band_start.reshape(-1)
    widths = band_width.reshape(-1)
    per_eye = N_ROW * N_COL
    zero = jnp.int32(0)

    def tile_step(carry, index):
        attended_all, dquery_all, cross_all, key_sum = carry
        view = (index // per_eye).astype(jnp.int32)
        slab = ((index // N_COL) % N_ROW).astype(jnp.int32)
        panel = (index % N_COL).astype(jnp.int32)
        other = (1 - view).astype(jnp.int32)
        first = starts[index].astype(jnp.int32)
        span = widths[index].astype(jnp.int32)
        row0 = (slab * TILE_ROWS).astype(jnp.int32)
        col0 = (panel * TILE_COLS).astype(jnp.int32)
        tile_q = lax.dynamic_slice(query, (view, row0, zero, col0), (1, TILE_ROWS, CH, TILE_COLS))[0]
        tile_g = lax.dynamic_slice(cotangent, (view, row0, zero, col0), (1, TILE_ROWS, CH, TILE_COLS))[0]
        band_k = lax.dynamic_slice(key, (other, row0, zero, first), (1, TILE_ROWS, CH, BAND_COLS))[0]
        band_v = lax.dynamic_slice(feat, (other, row0, zero, first), (1, TILE_ROWS, CH, BAND_COLS))[0]
        attended, dquery, dkey, dvalue = attend(tile_q, tile_g, band_k, band_v, span, scale)
        dkey_b = dkey.astype(jnp.bfloat16).astype(jnp.float32)
        cross_part = (dvalue + jnp.einsum('io,hoj->hij', wkey, dkey_b)).astype(jnp.bfloat16).astype(jnp.float32)
        key_sum = key_sum + jnp.einsum('hij,hoj->io', band_v.astype(jnp.float32), dkey_b)
        attended_all = lax.dynamic_update_slice(attended_all, attended[None], (view, row0, zero, col0))
        dquery_all = lax.dynamic_update_slice(dquery_all, dquery[None], (view, row0, zero, col0))
        current = lax.dynamic_slice(cross_all, (other, row0, zero, first), (1, TILE_ROWS, CH, BAND_COLS))
        cross_all = lax.dynamic_update_slice(cross_all, current + cross_part[None], (other, row0, zero, first))
        return (attended_all, dquery_all, cross_all, key_sum), None

    blank = jnp.zeros(images.shape, jnp.float32)
    init = (blank, blank, blank, jnp.zeros((CH, CH), jnp.float32))
    (attended_all, dquery_all, cross_all, key_grad), _ = lax.scan(tile_step, init, jnp.arange(2 * per_eye, dtype=jnp.int32))
    refined = (featf + attended_all).astype(jnp.bfloat16)
    dquery_b = dquery_all.astype(jnp.bfloat16).astype(jnp.float32)
    dfeat = cotangent.astype(jnp.float32) + jnp.einsum('io,ehow->ehiw', wquery, dquery_b) + cross_all
    dconv = (dfeat * slope(conv)).astype(jnp.bfloat16)
    dpad = jnp.pad(dconv, ((0, 0), (1, 1), (0, 0), (1, 1))).astype(jnp.float32)
    back = dfeat
    grads = []
    for a in range(3):
        line = []
        for b in range(3):
            back = back + jnp.einsum('io,ehow->ehiw', wconv[a, b], dpad[:, 2 - a:2 - a + height, :, 2 - b:2 - b + width_all])
            line.append(jnp.einsum('ehiw,ehow->io', padded[:, a:a + height, :, b:b + width_all], dconv.astype(jnp.float32)))
        grads.append(jnp.stack(line))
    conv_grad = jnp.stack(grads)
    query_grad = jnp.einsum('ehiw,ehow->io', featf, dquery_b)
    return refined, back.astype(jnp.bfloat16), conv_grad, query_grad, key_grad
```

```python
import functools

import jax
import jax.numpy as jnp
from jax import lax
from jax.experimental import pallas as pl
from jax.experimental.pallas import tpu as pltpu
from jax.sharding import PartitionSpec as P

BAND_PANELS = 4


def with_halo(block, sides, width):
    for axis, dim in sides:
        count = lax.axis_size(axis)
        forward = [(i, i + 1) for i in range(count - 1)]
        backward = [(target, source) for source, target in forward]
        low = lax.ppermute(
            lax.slice_in_dim(block, block.shape[dim] - width, None, axis=dim), axis, forward
        )
        high = lax.ppermute(lax.slice_in_dim(block, 0, width, axis=dim), axis, backward)
        block = jnp.concatenate([low, block, high], axis=dim)
    return block


def leaky(value):
    return jnp.where(value > 0, value, 0.1 * value)


def dot(lhs, rhs, dims):
    return lax.dot_general(lhs, rhs, (dims, ((), ())), preferred_element_type=jnp.float32)


NN = ((1,), (0,))
NT = ((1,), (1,))
TN = ((0,), (0,))


def attend_kernel(
    scale, live_ref, wq_ref, wk_ref, feat_ref, grad_ref, v0_ref, v1_ref, v2_ref, v3_ref,
    refined_ref, part_ref, x0_ref, x1_ref, x2_ref, x3_ref, qsum_ref, ksum_ref,
):
    values = (v0_ref, v1_ref, v2_ref, v3_ref)
    crosses = (x0_ref, x1_ref, x2_ref, x3_ref)
    cols = feat_ref.shape[2]
    wq = wq_ref[...]
    wk = wk_ref[...]
    wq_t = wq.T
    wk_t = wk.T

    @pl.when(pl.program_id(0) == 0)
    def _():
        qsum_ref[...] = jnp.zeros_like(qsum_ref)
        ksum_ref[...] = jnp.zeros_like(ksum_ref)

    qsum = jnp.zeros(qsum_ref.shape, jnp.float32)
    ksum = jnp.zeros(ksum_ref.shape, jnp.float32)
    for h in range(feat_ref.shape[0]):
        feat = feat_ref[h]
        grad = grad_ref[h]
        value = jnp.concatenate([ref[h] for ref in values], axis=1)
        key = dot(wk_t, value, NN).astype(jnp.bfloat16)
        query = dot(wq_t, feat, NN).astype(jnp.bfloat16)
        query_t = dot(feat.T, wq, NN).astype(jnp.bfloat16)
        score = dot(query_t, key, NN) * scale
        score = jnp.concatenate(
            [
                jnp.where(live_ref[o] > 0, score[:, o * cols : (o + 1) * cols], -jnp.inf)
                for o in range(BAND_PANELS)
            ],
            axis=1,
        )
        peak = jnp.max(score, axis=1, keepdims=True)
        expo = jnp.exp(score - peak)
        prob = expo * (1.0 / jnp.sum(expo, axis=1, keepdims=True))
        prob_b = prob.astype(jnp.bfloat16)
        dprob = dot(grad.T, value, NN)
        delta = jnp.sum(prob * dprob, axis=1, keepdims=True)
        dscore = (scale * prob * (dprob - delta)).astype(jnp.bfloat16)
        attended = dot(value, prob_b, NT)
        refined_ref[h] = (feat.astype(jnp.float32) + attended).astype(jnp.bfloat16)
        dquery = dot(key, dscore, NT).astype(jnp.bfloat16)
        dkey = dot(query, dscore, NN).astype(jnp.bfloat16)
        cross = (dot(grad, prob_b, NN) + dot(wk, dkey, NN)).astype(jnp.bfloat16)
        for o in range(BAND_PANELS):
            crosses[o][h] = cross[:, o * cols : (o + 1) * cols]
        part_ref[h] = grad.astype(jnp.float32) + dot(wq, dquery, NN)
        qsum = qsum + dot(feat, dquery, NT)
        ksum = ksum + dot(value, dkey, NT)
    qsum_ref[...] += qsum
    ksum_ref[...] += ksum


def attend(live, wq, wk, feat, grad, values, block_rows=4):
    rows, chans, cols = feat.shape
    tile = pl.BlockSpec((block_rows, chans, cols), lambda i: (i, 0, 0))
    square = pl.BlockSpec((chans, chans), lambda i: (0, 0))
    tile_b = jax.ShapeDtypeStruct((rows, chans, cols), jnp.bfloat16)
    tile_f = jax.ShapeDtypeStruct((rows, chans, cols), jnp.float32)
    square_f = jax.ShapeDtypeStruct((chans, chans), jnp.float32)
    flops = 2 * rows * chans * cols * cols * BAND_PANELS * 7
    return pl.pallas_call(
        functools.partial(attend_kernel, chans ** -0.5),
        grid=(rows // block_rows,),
        in_specs=[pl.BlockSpec(memory_space=pltpu.SMEM), square, square] + [tile] * 6,
        out_specs=[tile] * 6 + [square, square],
        out_shape=[tile_b, tile_f] + [tile_b] * 4 + [square_f, square_f],
        compiler_params=pltpu.CompilerParams(vmem_limit_bytes=48 * 1024 * 1024),
        cost_estimate=pl.CostEstimate(
            flops=flops, bytes_accessed=13 * rows * chans * cols * 2, transcendentals=rows * cols * cols * 4
        ),
    )(live, wq, wk, feat, grad, *values)


def along_y(block, shift, ny, nz):
    perm = [(y * nz + z, ((y + shift) % ny) * nz + z) for y in range(ny) for z in range(nz)]
    return lax.ppermute(block, "col", perm)


def across(block, shift, ny, nz):
    perm = [
        (e * ny * nz + y * nz + z, (1 - e) * ny * nz + y * nz + (z + shift) % nz)
        for e in range(2)
        for y in range(ny)
        for z in range(nz)
    ]
    return lax.ppermute(block, ("eye", "col"), perm)


def sum_all(total):
    total = total + lax.ppermute(total, "eye", [(0, 1), (1, 0)])
    n_row = lax.axis_size("row")
    n_col = lax.axis_size("col")
    lines, lanes = total.shape
    pieces = lax.all_to_all(total.reshape(n_row, lines // n_row, lanes), "row", 0, 0)
    piece = jnp.sum(pieces, axis=0)
    spread = lax.all_to_all(jnp.broadcast_to(piece[None], (n_col,) + piece.shape), "col", 0, 0)
    piece = jnp.sum(spread, axis=0)
    back = lax.all_to_all(jnp.broadcast_to(piece[None], (n_row,) + piece.shape), "row", 0, 0)
    return back.reshape(lines, lanes)


def body(images, cotangent, conv_weight, query_weight, key_weight, band_start, band_width):
    source = images[0]
    grad_out = cotangent[0]
    rows, chans, cols = source.shape
    nz = BAND_PANELS
    ny = lax.axis_size("col") // nz
    col = lax.axis_index("col")
    eye = lax.axis_index("eye")
    my_y = col // nz
    my_z = col % nz
    panel = band_start[0, 0, 0] // cols
    width = band_width[0, 0, 0]
    starts = lax.all_gather(band_start.reshape(1) // cols, ("eye", "col"), axis=0, tiled=True)

    padded = with_halo(source, (("row", 0), ("col", 2)), 1)
    conv = jnp.zeros((rows, chans, cols), jnp.float32)
    for a in range(3):
        for b in range(3):
            conv = conv + jnp.einsum(
                "io,hiw->how",
                conv_weight[a, b],
                padded[a : a + rows, :, b : b + cols],
                preferred_element_type=jnp.float32,
            )
    feat = (source.astype(jnp.float32) + leaky(conv)).astype(jnp.bfloat16)

    held = [feat] + [along_y(feat, shift, ny, nz) for shift in range(1, ny)]
    picks = []
    values = []
    for shift in range(nz):
        target = lax.dynamic_index_in_dim(
            starts, (1 - eye) * ny * nz + my_y * nz + (my_z + shift) % nz, 0, False
        )
        wanted = target + (my_z - target) % nz
        pick = (my_y - wanted // nz) % ny
        picks.append(pick)
        chosen = held[0]
        for k in range(1, ny):
            chosen = jnp.where(pick == k, held[k], chosen)
        values.append(across(chosen, shift, ny, nz))
    place = (my_z - jnp.arange(nz, dtype=jnp.int32) - panel) % nz
    live = (place * cols < width).astype(jnp.int32)

    refined, part, *crosses, query_local, key_local = attend(
        live, query_weight, key_weight, feat, grad_out, values
    )

    returned = [
        across(crosses[shift], -shift, ny, nz).astype(jnp.float32) for shift in range(nz)
    ]
    cross = part
    for k in range(ny):
        total = jnp.zeros((rows, chans, cols), jnp.float32)
        for shift in range(nz):
            total = total + jnp.where(picks[shift] == k, returned[shift], 0.0)
        if k > 0:
            total = along_y(total.astype(jnp.bfloat16), -k, ny, nz).astype(jnp.float32)
        cross = cross + total
    dfeat = cross
    dconv = (dfeat * jnp.where(conv > 0, 1.0, 0.1)).astype(jnp.bfloat16)
    dpad = with_halo(dconv, (("row", 0), ("col", 2)), 1)
    back = dfeat
    grads = []
    for a in range(3):
        for b in range(3):
            back = back + jnp.einsum(
                "io,how->hiw",
                conv_weight[a, b],
                dpad[2 - a : 2 - a + rows, :, 2 - b : 2 - b + cols],
                preferred_element_type=jnp.float32,
            )
            grads.append(
                jnp.einsum(
                    "hiw,how->io",
                    padded[a : a + rows, :, b : b + cols],
                    dconv,
                    preferred_element_type=jnp.float32,
                )
            )
    total = sum_all(jnp.concatenate(grads + [query_local, key_local], axis=0))
    total = total.reshape(11, chans, chans)
    conv_grad = total[:9].reshape(3, 3, chans, chans)
    return (refined[None], back.astype(jnp.bfloat16)[None], conv_grad, total[9], total[10])


def solution(mesh):
    return jax.shard_map(
        body,
        mesh=mesh,
        in_specs=(
            P("eye", "row", None, "col"),
            P("eye", "row", None, "col"),
            P(),
            P(),
            P(),
            P("eye", "row", "col"),
            P("eye", "row", "col"),
        ),
        out_specs=(P("eye", "row", None, "col"), P("eye", "row", None, "col"), P(), P(), P()),
        check_vma=False,
    )
```

```python
import functools

import jax
import jax.numpy as jnp
from jax import lax
from jax.experimental import pallas as pl
from jax.experimental.pallas import tpu as pltpu
from jax.sharding import PartitionSpec as P

BAND_PANELS = 4
LOG2E = 1.4426950408889634


def shifted(block, axis, step):
    count = lax.axis_size(axis)
    moved = lax.ppermute(block, axis, [(i, (i + step) % count) for i in range(count)])
    edge = 0 if step > 0 else count - 1
    return jnp.where(lax.axis_index(axis) == edge, jnp.zeros_like(moved), moved)


def with_halo(block):
    up = shifted(block[-1:], "row", 1)
    down = shifted(block[:1], "row", -1)
    block = jnp.concatenate([up, block, down], axis=0)
    left = shifted(block[:, :, -1], "col", 1)
    right = shifted(block[:, :, 0], "col", -1)
    return jnp.concatenate([left[:, :, None], block, right[:, :, None]], axis=2)


def leaky(value):
    return jnp.where(value > 0, value, 0.1 * value)


def dot(lhs, rhs, dims):
    return lax.dot_general(lhs, rhs, (dims, ((), ())), preferred_element_type=jnp.float32)


NN = ((1,), (0,))
NT = ((1,), (1,))
TN = ((0,), (0,))


def attend_kernel(
    scale, live_ref, wq_ref, wk_ref, feat_ref, grad_ref, v0_ref, v1_ref, v2_ref, v3_ref,
    refined_ref, part_ref, x0_ref, x1_ref, x2_ref, x3_ref, qsum_ref, ksum_ref,
):
    values = (v0_ref, v1_ref, v2_ref, v3_ref)
    crosses = (x0_ref, x1_ref, x2_ref, x3_ref)
    rows, chans, cols = feat_ref.shape
    wq = wq_ref[...]
    wk = wk_ref[...]
    wq_t = wq.T
    wk_t = wk.T

    @pl.when(pl.program_id(0) == 0)
    def _():
        qsum_ref[...] = jnp.zeros_like(qsum_ref)
        ksum_ref[...] = jnp.zeros_like(ksum_ref)

    feat_all = jnp.concatenate([feat_ref[h] for h in range(rows)], axis=1)
    query_all = dot(wq_t, feat_all, NN).astype(jnp.bfloat16)
    keyed_all = dot(wk, query_all, NN) * scale
    keyed_b = keyed_all.astype(jnp.bfloat16)
    keyed_2 = (keyed_all * LOG2E).astype(jnp.bfloat16)
    moved = []
    for h in range(rows):
        at = slice(h * cols, (h + 1) * cols)
        grad = grad_ref[h]
        value = jnp.concatenate([ref[h] for ref in values], axis=1)
        pair = dot(jnp.concatenate([keyed_2[:, at], grad], axis=1).T, value, NN)
        score = jnp.concatenate(
            [
                jnp.where(live_ref[o] > 0, pair[:cols, o * cols : (o + 1) * cols], -jnp.inf)
                for o in range(BAND_PANELS)
            ],
            axis=1,
        )
        dprob = pair[cols:]
        expo = jnp.exp2(score - jnp.max(score, axis=1, keepdims=True))
        prob = expo * (1.0 / jnp.sum(expo, axis=1, keepdims=True))
        delta = jnp.sum(prob * dprob, axis=1, keepdims=True)
        dscore = prob * (dprob - delta)
        both = jnp.concatenate([prob.astype(jnp.bfloat16), dscore.astype(jnp.bfloat16)], axis=0)
        cross = dot(jnp.concatenate([grad, keyed_b[:, at]], axis=1), both, NN).astype(jnp.bfloat16)
        for o in range(BAND_PANELS):
            crosses[o][h] = cross[:, o * cols : (o + 1) * cols]
        summed = dot(both, value.T, NN).T
        refined_ref[h] = (feat_ref[h].astype(jnp.float32) + summed[:, :cols]).astype(jnp.bfloat16)
        moved.append((summed[:, cols:] * scale).astype(jnp.bfloat16))
    moved_all = jnp.concatenate(moved, axis=1)
    dquery = dot(wk_t, moved_all, NN).astype(jnp.bfloat16)
    part = dot(wq, dquery, NN)
    for h in range(rows):
        part_ref[h] = grad_ref[h].astype(jnp.float32) + part[:, h * cols : (h + 1) * cols]
    qsum_ref[...] += dot(feat_all, dquery, NT)
    ksum_ref[...] += dot(moved_all, query_all, NT)


def attend(live, wq, wk, feat, grad, values, block_rows=5):
    rows, chans, cols = feat.shape
    tile = pl.BlockSpec((block_rows, chans, cols), lambda i: (i, 0, 0))
    square = pl.BlockSpec((chans, chans), lambda i: (0, 0))
    tile_b = jax.ShapeDtypeStruct((rows, chans, cols), jnp.bfloat16)
    tile_f = jax.ShapeDtypeStruct((rows, chans, cols), jnp.float32)
    square_f = jax.ShapeDtypeStruct((chans, chans), jnp.float32)
    flops = 2 * rows * chans * cols * cols * BAND_PANELS * 6
    return pl.pallas_call(
        functools.partial(attend_kernel, chans ** -0.5),
        grid=(rows // block_rows,),
        in_specs=[pl.BlockSpec(memory_space=pltpu.SMEM), square, square] + [tile] * 6,
        out_specs=[tile] * 6 + [square, square],
        out_shape=[tile_b, tile_f] + [tile_b] * 4 + [square_f, square_f],
        compiler_params=pltpu.CompilerParams(vmem_limit_bytes=48 * 1024 * 1024),
        cost_estimate=pl.CostEstimate(
            flops=flops, bytes_accessed=13 * rows * chans * cols * 2, transcendentals=rows * cols * cols * 4
        ),
    )(live, wq, wk, feat, grad, *values)


def along_y(block, shift, ny, nz):
    perm = [(y * nz + z, ((y + shift) % ny) * nz + z) for y in range(ny) for z in range(nz)]
    return lax.ppermute(block, "col", perm)


def across(block, shift, ny, nz):
    perm = [
        (e * ny * nz + y * nz + z, (1 - e) * ny * nz + y * nz + (z + shift) % nz)
        for e in range(2)
        for y in range(ny)
        for z in range(nz)
    ]
    return lax.ppermute(block, ("eye", "col"), perm)


def sum_all(pieces):
    chans = pieces[0].shape[0]
    pieces = pieces + [jnp.zeros_like(pieces[0])] * (-len(pieces) % 4)
    pairs = [jnp.concatenate(pieces[i : i + 2], axis=1) for i in range(0, len(pieces), 2)]
    count = len(pairs) // 2
    lower = jnp.concatenate(pairs[:count], axis=0)
    upper = jnp.concatenate(pairs[count:], axis=0)
    first = lax.axis_index("eye") == 0
    swap = [(0, 1), (1, 0)]
    total = jnp.where(first, lower, upper) + lax.ppermute(
        jnp.where(first, upper, lower), "eye", swap
    )
    for axis, outer, inner in (("row", 1, 0), ("col", 0, 1), ("row", 0, 1), ("col", 1, 0)):
        size = lax.axis_size(axis)
        low = BAND_PANELS if axis == "col" else max(size // 2, 1)
        high = size // low
        steps = low if outer else high
        terms = []
        for step in range(1, steps):
            if outer:
                perm = [(h * low + i, h * low + (i + step) % low) for h in range(high) for i in range(low)]
            else:
                perm = [(h * low + i, (h + step) % high * low + i) for h in range(high) for i in range(low)]
            terms.append(lax.ppermute(total, axis, perm))
        total = sum(terms, total)
    other = lax.ppermute(total, "eye", swap)
    both = jnp.concatenate([jnp.where(first, total, other), jnp.where(first, other, total)], axis=0)
    both = both.reshape(-1, chans, 2, chans)
    return [both[i // 2, :, i % 2] for i in range(2 * both.shape[0])]


def body(images, cotangent, conv_weight, query_weight, key_weight, band_start, band_width):
    source = images[0]
    grad_out = cotangent[0]
    rows, chans, cols = source.shape
    nz = BAND_PANELS
    ny = lax.axis_size("col") // nz
    col = lax.axis_index("col")
    my_y = col // nz
    my_z = col % nz
    panel = band_start[0, 0, 0] // cols
    width = band_width[0, 0, 0]
    targets = [across(panel.reshape(1, 1), -shift, ny, nz)[0, 0] for shift in range(nz)]
    picks = []
    for target in targets:
        wanted = target + (my_z - target) % nz
        picks.append((my_y - wanted // nz) % ny)
    place = (my_z - jnp.arange(nz, dtype=jnp.int32) - panel) % nz
    live = (place * cols < width).astype(jnp.int32)

    padded = with_halo(source)
    conv = jnp.zeros((rows, chans, cols), jnp.float32)
    for a in range(3):
        for b in range(3):
            conv = conv + jnp.einsum(
                "io,hiw->how",
                conv_weight[a, b],
                padded[a : a + rows, :, b : b + cols],
                preferred_element_type=jnp.float32,
            )
    feat = (source.astype(jnp.float32) + leaky(conv)).astype(jnp.bfloat16)

    chunks = [slice(0, rows // 2), slice(rows // 2, rows)]
    refined = []
    dfeats = []
    query_local = 0.0
    key_local = 0.0
    for at in chunks:
        piece = feat[at]
        held = [piece] + [along_y(piece, shift, ny, nz) for shift in range(1, ny)]
        values = []
        for shift in range(nz):
            chosen = held[0]
            for k in range(1, ny):
                chosen = jnp.where(picks[shift] == k, held[k], chosen)
            values.append(across(chosen, shift, ny, nz))
        done, part, *crosses, query_part, key_part = attend(
            live, query_weight, key_weight, piece, grad_out[at], values
        )
        refined.append(done)
        query_local = query_local + query_part
        key_local = key_local + key_part
        returned = [
            across(crosses[shift], -shift, ny, nz).astype(jnp.float32) for shift in range(nz)
        ]
        for k in range(ny):
            total = jnp.zeros(piece.shape, jnp.float32)
            for shift in range(nz):
                total = total + jnp.where(picks[shift] == k, returned[shift], 0.0)
            if k > 0:
                total = along_y(total.astype(jnp.bfloat16), -k, ny, nz).astype(jnp.float32)
            part = part + total
        dfeats.append(part)
    refined = jnp.concatenate(refined, axis=0)
    dfeat = jnp.concatenate(dfeats, axis=0)
    dconv = (dfeat * jnp.where(conv > 0, 1.0, 0.1)).astype(jnp.bfloat16)
    grads = [
        jnp.einsum(
            "hiw,how->io",
            padded[a : a + rows, :, b : b + cols],
            dconv,
            preferred_element_type=jnp.float32,
        )
        for a in range(3)
        for b in range(3)
    ]
    total = sum_all(grads + [query_local, key_local])
    dpad = with_halo(dconv)
    back = dfeat
    for a in range(3):
        for b in range(3):
            back = back + jnp.einsum(
                "io,how->hiw",
                conv_weight[a, b],
                dpad[2 - a : 2 - a + rows, :, 2 - b : 2 - b + cols],
                preferred_element_type=jnp.float32,
            )
    conv_grad = jnp.stack(total[:9]).reshape(3, 3, chans, chans)
    return (refined[None], back.astype(jnp.bfloat16)[None], conv_grad, total[9], total[10])


def solution(mesh):
    return jax.shard_map(
        body,
        mesh=mesh,
        in_specs=(
            P("eye", "row", None, "col"),
            P("eye", "row", None, "col"),
            P(),
            P(),
            P(),
            P("eye", "row", "col"),
            P("eye", "row", "col"),
        ),
        out_specs=(P("eye", "row", None, "col"), P("eye", "row", None, "col"), P(), P(), P()),
        check_vma=False,
    )
```

```python
import functools

import jax
import jax.numpy as jnp
from jax import lax
from jax.experimental import pallas as pl
from jax.experimental.pallas import tpu as pltpu
from jax.sharding import PartitionSpec as P

BAND_PANELS = 4
LOG2E = 1.4426950408889634


def shifted(block, axis, step):
    count = lax.axis_size(axis)
    moved = lax.ppermute(block, axis, [(i, (i + step) % count) for i in range(count)])
    edge = 0 if step > 0 else count - 1
    return jnp.where(lax.axis_index(axis) == edge, jnp.zeros_like(moved), moved)


def row_halo(block):
    up = shifted(block[-1:], "row", 1)
    down = shifted(block[:1], "row", -1)
    return jnp.concatenate([up, block, down], axis=0)


def with_columns(left, block, right):
    return jnp.concatenate([left[:, :, None], block, right[:, :, None]], axis=2)


def leaky(value):
    return jnp.where(value > 0, value, 0.1 * value)


def dot(lhs, rhs, dims):
    return lax.dot_general(lhs, rhs, (dims, ((), ())), preferred_element_type=jnp.float32)


NN = ((1,), (0,))
NT = ((1,), (1,))
TN = ((0,), (0,))


def attend_kernel(
    scale, live_ref, wq_ref, wk_ref, feat_ref, grad_ref, v0_ref, v1_ref, v2_ref, v3_ref,
    refined_ref, part_ref, x0_ref, x1_ref, x2_ref, x3_ref, qsum_ref, ksum_ref,
):
    values = (v0_ref, v1_ref, v2_ref, v3_ref)
    crosses = (x0_ref, x1_ref, x2_ref, x3_ref)
    rows, chans, cols = feat_ref.shape
    wq = wq_ref[...]
    wk = wk_ref[...]
    wq_t = wq.T
    wk_t = wk.T

    @pl.when(pl.program_id(0) == 0)
    def _():
        qsum_ref[...] = jnp.zeros_like(qsum_ref)
        ksum_ref[...] = jnp.zeros_like(ksum_ref)

    feat_all = jnp.concatenate([feat_ref[h] for h in range(rows)], axis=1)
    query_all = dot(wq_t, feat_all, NN).astype(jnp.bfloat16)
    keyed_all = dot(wk, query_all, NN) * scale
    keyed_b = keyed_all.astype(jnp.bfloat16)
    keyed_2 = (keyed_all * LOG2E).astype(jnp.bfloat16)
    moved = []
    for h in range(rows):
        at = slice(h * cols, (h + 1) * cols)
        grad = grad_ref[h]
        value = jnp.concatenate([ref[h] for ref in values], axis=1)
        pair = dot(jnp.concatenate([keyed_2[:, at], grad], axis=1).T, value, NN)
        score = jnp.concatenate(
            [
                jnp.where(live_ref[o] > 0, pair[:cols, o * cols : (o + 1) * cols], -jnp.inf)
                for o in range(BAND_PANELS)
            ],
            axis=1,
        )
        dprob = pair[cols:]
        expo = jnp.exp2(score - jnp.max(score, axis=1, keepdims=True))
        prob = expo * (1.0 / jnp.sum(expo, axis=1, keepdims=True))
        delta = jnp.sum(prob * dprob, axis=1, keepdims=True)
        dscore = prob * (dprob - delta)
        both = jnp.concatenate([prob.astype(jnp.bfloat16), dscore.astype(jnp.bfloat16)], axis=0)
        cross = dot(jnp.concatenate([grad, keyed_b[:, at]], axis=1), both, NN).astype(jnp.bfloat16)
        for o in range(BAND_PANELS):
            crosses[o][h] = cross[:, o * cols : (o + 1) * cols]
        summed = dot(both, value.T, NN).T
        refined_ref[h] = (feat_ref[h].astype(jnp.float32) + summed[:, :cols]).astype(jnp.bfloat16)
        moved.append((summed[:, cols:] * scale).astype(jnp.bfloat16))
    moved_all = jnp.concatenate(moved, axis=1)
    dquery = dot(wk_t, moved_all, NN).astype(jnp.bfloat16)
    part = dot(wq, dquery, NN)
    for h in range(rows):
        part_ref[h] = grad_ref[h].astype(jnp.float32) + part[:, h * cols : (h + 1) * cols]
    qsum_ref[...] += dot(feat_all, dquery, NT)
    ksum_ref[...] += dot(moved_all, query_all, NT)


def attend(live, wq, wk, feat, grad, values, block_rows=5):
    rows, chans, cols = feat.shape
    tile = pl.BlockSpec((block_rows, chans, cols), lambda i: (i, 0, 0))
    square = pl.BlockSpec((chans, chans), lambda i: (0, 0))
    tile_b = jax.ShapeDtypeStruct((rows, chans, cols), jnp.bfloat16)
    tile_f = jax.ShapeDtypeStruct((rows, chans, cols), jnp.float32)
    square_f = jax.ShapeDtypeStruct((chans, chans), jnp.float32)
    flops = 2 * rows * chans * cols * cols * BAND_PANELS * 6
    return pl.pallas_call(
        functools.partial(attend_kernel, chans ** -0.5),
        grid=(rows // block_rows,),
        in_specs=[pl.BlockSpec(memory_space=pltpu.SMEM), square, square] + [tile] * 6,
        out_specs=[tile] * 6 + [square, square],
        out_shape=[tile_b, tile_f] + [tile_b] * 4 + [square_f, square_f],
        compiler_params=pltpu.CompilerParams(vmem_limit_bytes=48 * 1024 * 1024),
        cost_estimate=pl.CostEstimate(
            flops=flops, bytes_accessed=13 * rows * chans * cols * 2, transcendentals=rows * cols * cols * 4
        ),
    )(live, wq, wk, feat, grad, *values)


def permute(block, axis, shift, ny, nz):
    if axis == "y":
        perm = [(y * nz + z, ((y + shift) % ny) * nz + z) for y in range(ny) for z in range(nz)]
    else:
        perm = [(y * nz + z, y * nz + (z + shift) % nz) for y in range(ny) for z in range(nz)]
    return lax.ppermute(block, "col", perm)


def across(block, shift, ny, nz):
    perm = [
        (e * ny * nz + y * nz + z, (1 - e) * ny * nz + y * nz + (z + shift) % nz)
        for e in range(2)
        for y in range(ny)
        for z in range(nz)
    ]
    return lax.ppermute(block, ("eye", "col"), perm)


def swap_eyes(block):
    return lax.ppermute(block, "eye", [(0, 1), (1, 0)])


def sum_four(block, send):
    block = block.astype(jnp.bfloat16)
    near, far, last = [send(block, step).astype(jnp.float32) for step in (1, 2, 3)]
    return (block.astype(jnp.float32) + far) + (near + last)


def sum_x(block):
    low = lax.axis_size("row") // 2
    if low == 1:
        return block
    perms = [[(i, i // low * low + (i + step) % low) for i in range(2 * low)] for step in range(4)]
    return sum_four(block, lambda value, step: lax.ppermute(value, "row", perms[step]))


def sum_far(block):
    size = lax.axis_size("row")
    block = block.astype(jnp.bfloat16)
    other = lax.ppermute(block, "row", [(i, (i + size // 2) % size) for i in range(size)])
    return block.astype(jnp.float32) + other.astype(jnp.float32)


def split_eyes(pieces):
    pieces = pieces + [jnp.zeros_like(pieces[0])] * (-len(pieces) % 4)
    half = len(pieces) // 2
    wide = jnp.concatenate(
        [jnp.concatenate(pieces[:half], axis=0), jnp.concatenate(pieces[half:], axis=0)], axis=1
    )
    rows = wide.shape[0] // 2
    first = lax.axis_index("eye") == 0
    lower, upper = wide[:rows], wide[rows:]
    return jnp.where(first, lower, upper), jnp.where(first, upper, lower)


def join_eyes(total):
    chans = total.shape[1] // 2
    first = lax.axis_index("eye") == 0
    other = swap_eyes(total)
    wide = jnp.concatenate([jnp.where(first, total, other), jnp.where(first, other, total)], axis=0)
    half = wide.shape[0] // chans
    return jnp.concatenate(
        [wide[:, :chans].reshape(half, chans, chans), wide[:, chans:].reshape(half, chans, chans)]
    )


def body(images, cotangent, conv_weight, query_weight, key_weight, band_start, band_width):
    source = images[0]
    grad_out = cotangent[0]
    rows, chans, cols = source.shape
    nz = BAND_PANELS
    ny = lax.axis_size("col") // nz
    col = lax.axis_index("col")
    my_y = col // nz
    my_z = col % nz
    panel = band_start[0, 0, 0] // cols
    width = band_width[0, 0, 0]
    mark = jnp.full((1, cols), panel)
    known = [across(mark, -shift, ny, nz) for shift in (0, 1)]
    padded, *known = lax.optimization_barrier((row_halo(source), *known))
    known = known + [across(mark, -shift, ny, nz) for shift in (2, 3)]
    left = shifted(padded[:, :, -1], "col", 1)
    right = shifted(padded[:, :, 0], "col", -1)
    left, right, *known = lax.optimization_barrier((left, right, *known))
    padded = with_columns(left, padded, right)
    picks = []
    for shift in range(nz):
        target = known[shift][0, 0]
        wanted = target + (my_z - target) % nz
        picks.append((my_y - wanted // nz) % ny)
    place = (my_z - jnp.arange(nz, dtype=jnp.int32) - panel) % nz
    live = (place * cols < width).astype(jnp.int32)

    conv = jnp.zeros((rows, chans, cols), jnp.float32)
    for a in range(3):
        for b in range(3):
            conv = conv + jnp.einsum(
                "io,hiw->how",
                conv_weight[a, b],
                padded[a : a + rows, :, b : b + cols],
                preferred_element_type=jnp.float32,
            )
    feat = (source.astype(jnp.float32) + leaky(conv)).astype(jnp.bfloat16)

    chunks = [slice(0, rows // 2), slice(rows // 2, rows)]
    refined = []
    dfeats = []
    query_local = 0.0
    key_local = 0.0
    held = [feat] + [permute(feat, "y", shift, ny, nz) for shift in range(1, ny)]
    chosen = []
    for at in chunks:
        for shift in range(nz):
            one = held[0][at]
            for k in range(1, ny):
                one = jnp.where(picks[shift] == k, held[k][at], one)
            chosen.append(one)
    chosen = list(lax.optimization_barrier(tuple(chosen)))
    for i, at in enumerate(chunks):
        piece = feat[at]
        sent = chosen[i * nz : (i + 1) * nz]
        if i > 0:
            *sent, _ = lax.optimization_barrier((*sent, values[0]))
        values = [across(sent[shift], shift, ny, nz) for shift in range(nz)]
        done, part, *crosses, query_part, key_part = attend(
            live, query_weight, key_weight, piece, grad_out[at], values
        )
        refined.append(done)
        query_local = query_local + query_part
        key_local = key_local + key_part
        returned = [
            across(crosses[shift], -shift, ny, nz).astype(jnp.float32) for shift in range(nz)
        ]
        for k in range(ny):
            total = jnp.zeros(piece.shape, jnp.float32)
            for shift in range(nz):
                total = total + jnp.where(picks[shift] == k, returned[shift], 0.0)
            if k > 0:
                total = permute(total.astype(jnp.bfloat16), "y", -k, ny, nz).astype(jnp.float32)
            part = part + total
        dfeats.append(part)
    refined = jnp.concatenate(refined, axis=0)
    dfeat = jnp.concatenate(dfeats, axis=0)
    dconv = (dfeat * jnp.where(conv > 0, 1.0, 0.1)).astype(jnp.bfloat16)
    grads = [
        jnp.einsum(
            "hiw,how->io",
            padded[a : a + rows, :, b : b + cols],
            dconv,
            preferred_element_type=jnp.float32,
        )
        for a in range(3)
        for b in range(3)
    ]
    mine, given = split_eyes(grads + [query_local, key_local])
    total = mine + swap_eyes(given)
    total, dpad = lax.optimization_barrier((total, row_halo(dconv)))
    left = shifted(dpad[:, :, -1], "col", 1)
    total, left = lax.optimization_barrier((sum_x(total), left))
    right = shifted(dpad[:, :, 0], "col", -1)
    total = sum_four(total, lambda value, step: permute(value, "y", step, ny, nz))
    total, right = lax.optimization_barrier((total, right))
    dpad = with_columns(left, dpad, right)
    total = sum_far(total)
    total = sum_four(total, lambda value, step: permute(value, "z", step, ny, nz))
    total = join_eyes(total)
    back = dfeat
    for a in range(3):
        for b in range(3):
            back = back + jnp.einsum(
                "io,how->hiw",
                conv_weight[a, b],
                dpad[2 - a : 2 - a + rows, :, 2 - b : 2 - b + cols],
                preferred_element_type=jnp.float32,
            )
    conv_grad = total[:9].reshape(3, 3, chans, chans)
    return (refined[None], back.astype(jnp.bfloat16)[None], conv_grad, total[9], total[10])


def solution(mesh):
    return jax.shard_map(
        body,
        mesh=mesh,
        in_specs=(
            P("eye", "row", None, "col"),
            P("eye", "row", None, "col"),
            P(),
            P(),
            P(),
            P("eye", "row", "col"),
            P("eye", "row", "col"),
        ),
        out_specs=(P("eye", "row", None, "col"), P("eye", "row", None, "col"), P(), P(), P()),
        check_vma=False,
    )
```

```python
import functools

import jax
import jax.numpy as jnp
from jax import lax
from jax.experimental import pallas as pl
from jax.experimental.pallas import tpu as pltpu
from jax.sharding import PartitionSpec as P

BAND_PANELS = 4
LOG2E = 1.4426950408889634


def shifted(block, axis, step):
    count = lax.axis_size(axis)
    moved = lax.ppermute(block, axis, [(i, (i + step) % count) for i in range(count)])
    edge = 0 if step > 0 else count - 1
    return jnp.where(lax.axis_index(axis) == edge, jnp.zeros_like(moved), moved)


def row_halo(block):
    up = shifted(block[-1:], "row", 1)
    down = shifted(block[:1], "row", -1)
    return jnp.concatenate([up, block, down], axis=0)


def edge_tile(left, right, cols):
    pad = ((0, 0), (0, cols // 2 - left.shape[0]))
    return jnp.concatenate([jnp.pad(left.T, pad), jnp.pad(right.T, pad)], axis=1)


def dot(lhs, rhs, dims):
    return lax.dot_general(lhs, rhs, (dims, ((), ())), preferred_element_type=jnp.float32)


NN = ((1,), (0,))
NT = ((1,), (1,))
TN = ((0,), (0,))


def with_columns(middle, edges, line):
    cols = middle.shape[1]
    lane = lax.broadcasted_iota(jnp.int32, middle.shape, 1)
    low = jnp.where(lane == 0, edges[:, line : line + 1], pltpu.roll(middle, 1, 1))
    at = cols // 2 + line
    high = jnp.where(lane == cols - 1, edges[:, at : at + 1], pltpu.roll(middle, cols - 1, 1))
    return jnp.concatenate([low, middle, high], axis=0).astype(jnp.bfloat16)


def back_kernel(taps_ref, dfeat_ref, up_ref, dconv_ref, down_ref, edge_ref, out_ref):
    rows, chans, cols = dfeat_ref.shape
    edges = edge_ref[...].astype(jnp.float32)
    tall = [up_ref[0]] + [dconv_ref[h] for h in range(rows)] + [down_ref[0]]
    wide = [with_columns(tall[r].astype(jnp.float32), edges, r) for r in range(rows + 2)]
    lines = dot(taps_ref[...], jnp.concatenate(wide, axis=1), NN)
    for h in range(rows):
        total = dfeat_ref[h]
        for a in range(3):
            at = (h + 2 - a) * cols
            total = total + lines[a * chans : (a + 1) * chans, at : at + cols]
        out_ref[h] = total.astype(jnp.bfloat16)


def convolve_back(taps, dfeat, up, dconv, down, edges):
    rows, chans, cols = dfeat.shape
    return pl.pallas_call(
        back_kernel,
        in_specs=[pl.BlockSpec(memory_space=pltpu.VMEM)] * 6,
        out_specs=pl.BlockSpec(memory_space=pltpu.VMEM),
        out_shape=jax.ShapeDtypeStruct(dfeat.shape, jnp.bfloat16),
        compiler_params=pltpu.CompilerParams(vmem_limit_bytes=24 * 1024 * 1024),
        cost_estimate=pl.CostEstimate(
            flops=2 * (rows + 2) * cols * 9 * chans * chans, bytes_accessed=10 * rows * chans * cols, transcendentals=0
        ),
    )(taps, dfeat, up, dconv, down, edges)


def attend_kernel(scale, first, rows, live_ref, wq_ref, wk_ref, wc_ref, grad_ref, own_ref, *refs):
    count = len(refs) - 8
    bands = [refs[o:count:BAND_PANELS] for o in range(BAND_PANELS)]
    refined_ref, part_ref, conv_ref, x0_ref, x1_ref, x2_ref, x3_ref, sums_ref = refs[count:]
    crosses = (x0_ref, x1_ref, x2_ref, x3_ref)
    chans, cols = own_ref.shape[1:]
    wq = wq_ref[...]
    wk = wk_ref[...]

    def image(source, line):
        for ref in source:
            if line < ref.shape[0]:
                return ref[line].astype(jnp.float32)
            line -= ref.shape[0]

    sources = [(own_ref,)] + bands
    edges = [image(source, 0) for source in sources]
    wide = [
        jnp.concatenate([
                with_columns(image(s, 1 + first + r), e, first + r) for s, e in zip(sources, edges)
            ], axis=1)
        for r in range(rows + 2)
    ]
    lines = [dot(wc_ref[...], block, NN) for block in wide]
    convs = [
        lines[h][:chans] + lines[h + 1][chans : 2 * chans] + lines[h + 2][2 * chans :]
        for h in range(rows)
    ]
    feats = [
        (
            wide[h + 1][chans : 2 * chans].astype(jnp.float32)
            + jnp.where(convs[h] > 0, convs[h], 0.1 * convs[h])
        ).astype(jnp.bfloat16)
        for h in range(rows)
    ]
    feat_all = jnp.concatenate([feat[:, :cols] for feat in feats], axis=1)
    value_rows = [feat[:, cols:] for feat in feats]
    query_all = dot(wq.T, feat_all, NN).astype(jnp.bfloat16)
    keyed_all = dot(wk, query_all, NN) * scale
    keyed_b = keyed_all.astype(jnp.bfloat16)
    keyed_2 = (keyed_all * LOG2E).astype(jnp.bfloat16)
    spans = [slice(h * cols, (h + 1) * cols) for h in range(rows)]

    pairs = [
        dot(jnp.concatenate([keyed_2[:, spans[h]], grad_ref[h]], axis=1).T, value_rows[h], NN)
        for h in range(rows)
    ]
    probs = []
    for pair in pairs:
        score = jnp.concatenate(
            [
                jnp.where(live_ref[o] > 0, pair[:cols, o * cols : (o + 1) * cols], -jnp.inf)
                for o in range(BAND_PANELS)
            ],
            axis=1,
        )
        dprob = pair[cols:]
        expo = jnp.exp2(score - jnp.max(score, axis=1, keepdims=True))
        prob = expo * (1.0 / jnp.sum(expo, axis=1, keepdims=True))
        delta = jnp.sum(prob * dprob, axis=1, keepdims=True)
        dscore = prob * (dprob - delta)
        probs.append(
            jnp.concatenate([prob.astype(jnp.bfloat16), dscore.astype(jnp.bfloat16)], axis=0)
        )
    moved = []
    passed = []
    for h in range(rows):
        lhs = jnp.concatenate([grad_ref[h], keyed_b[:, spans[h]]], axis=1)
        cross = dot(lhs, probs[h], NN)
        passed.append(cross)
        for o in range(BAND_PANELS):
            crosses[o][h] = cross[:, o * cols : (o + 1) * cols].astype(jnp.bfloat16)
        summed = dot(value_rows[h], probs[h], NT)
        refined_ref[h] = (feats[h][:, :cols].astype(jnp.float32) + summed[:, :cols]).astype(
            jnp.bfloat16
        )
        moved.append((summed[:, cols:] * scale).astype(jnp.bfloat16))
    moved_all = jnp.concatenate(moved, axis=1)
    dquery = dot(wk.T, moved_all, NN).astype(jnp.bfloat16)
    part_all = dot(wq, dquery, NN)
    shares = []
    for h in range(rows):
        part = grad_ref[h].astype(jnp.float32) + part_all[:, spans[h]]
        part_ref[h] = part
        conv_ref[h] = convs[h][:, :cols]
        share = jnp.concatenate([part, passed[h]], axis=1)
        shares.append((share * jnp.where(convs[h] > 0, 1.0, 0.1)).astype(jnp.bfloat16))
    none = jnp.zeros_like(shares[0])
    total = jnp.zeros((3 * chans, 3 * chans), jnp.float32)
    for r in range(rows + 2):
        taps = [shares[r - a] if 0 <= r - a < rows else none for a in range(3)]
        total = total + dot(wide[r], jnp.concatenate(taps, axis=0), NT)
    sums_ref[0] = total[:, : 2 * chans]
    square = jnp.concatenate([dot(feat_all, dquery, NT), dot(moved_all, query_all, NT)], axis=0)
    square = jnp.concatenate([square, jnp.zeros((chans, chans), jnp.float32)], axis=0)
    sums_ref[1] = jnp.concatenate([total[:, 2 * chans :], square], axis=1)


def attend(live, wq, wk, wc, grad, own, first, values):
    rows, chans, cols = grad.shape
    whole = pl.BlockSpec(memory_space=pltpu.VMEM)
    tile_b = jax.ShapeDtypeStruct((rows, chans, cols), jnp.bfloat16)
    tile_f = jax.ShapeDtypeStruct((rows, chans, cols), jnp.float32)
    sums = jax.ShapeDtypeStruct((2, 3 * chans, 2 * chans), jnp.float32)
    flops = 2 * rows * chans * cols * cols * BAND_PANELS * 12
    return pl.pallas_call(
        functools.partial(attend_kernel, chans ** -0.5, first, rows),
        in_specs=[pl.BlockSpec(memory_space=pltpu.SMEM)] + [whole] * (5 + len(values)),
        out_specs=[whole] * 8,
        out_shape=[tile_b, tile_f, tile_f] + [tile_b] * 4 + [sums],
        compiler_params=pltpu.CompilerParams(vmem_limit_bytes=24 * 1024 * 1024),
        cost_estimate=pl.CostEstimate(
            flops=flops, bytes_accessed=20 * rows * chans * cols * 2, transcendentals=rows * cols * cols * 4
        ),
    )(live, wq, wk, wc, grad, own, *values)


def permute(block, axis, shift, ny, nz):
    if axis == "y":
        perm = [(y * nz + z, ((y + shift) % ny) * nz + z) for y in range(ny) for z in range(nz)]
    else:
        perm = [(y * nz + z, y * nz + (z + shift) % nz) for y in range(ny) for z in range(nz)]
    return lax.ppermute(block, "col", perm)


def across(block, shift, ny, nz):
    perm = [
        (e * ny * nz + y * nz + z, (1 - e) * ny * nz + y * nz + (z + shift) % nz)
        for e in range(2)
        for y in range(ny)
        for z in range(nz)
    ]
    return lax.ppermute(block, ("eye", "col"), perm)


def swap_eyes(block):
    return lax.ppermute(block, "eye", [(0, 1), (1, 0)])


def sum_pair(block, axis, step):
    block = block.astype(jnp.bfloat16)
    size = lax.axis_size(axis)
    perm = [(i, i // (2 * step) * 2 * step + (i + step) % (2 * step)) for i in range(size)]
    other = lax.ppermute(block, axis, perm)
    return block.astype(jnp.float32) + other.astype(jnp.float32)


def sum_four(own, near, far, last):
    own, near, far, last = [value.astype(jnp.float32) for value in (own, near, far, last)]
    return (own + far) + (near + last)


def join_eyes(total):
    chans = total.shape[1] // 2
    first = lax.axis_index("eye") == 0
    other = swap_eyes(total)
    lower, upper = jnp.where(first, other, total), jnp.where(first, total, other)
    taps = [lower[:, :chans], lower[:, chans:], upper[:, :chans]]
    conv_grad = jnp.stack([tap.reshape(3, chans, chans) for tap in taps])
    return conv_grad, upper[:chans, chans:], upper[chans : 2 * chans, chans:]


def body(images, cotangent, conv_weight, query_weight, key_weight, band_start, band_width):
    source = images[0]
    grad_out = cotangent[0]
    rows, chans, cols = source.shape
    nz = BAND_PANELS
    ny = lax.axis_size("col") // nz
    col = lax.axis_index("col")
    my_y = col // nz
    my_z = col % nz
    panel = band_start[0, 0, 0] // cols
    width = band_width[0, 0, 0]
    padded = lax.optimization_barrier(row_halo(source))
    left = shifted(padded[:, :, -1], "col", 1)
    right = shifted(padded[:, :, 0], "col", -1)
    sheet = jnp.concatenate([edge_tile(left, right, cols)[None], padded], axis=0)
    sheet, mark = lax.optimization_barrier((sheet, jnp.full((1, cols), panel)))
    held = [sheet] + [permute(sheet, "y", shift, ny, nz) for shift in range(1, ny)]
    known = [across(mark, -shift, ny, nz) for shift in range(nz)]
    picks = []
    for shift in range(nz):
        target = known[shift][0, 0]
        wanted = target + (my_z - target) % nz
        picks.append((my_y - wanted // nz) % ny)
    place = (my_z - jnp.arange(nz, dtype=jnp.int32) - panel) % nz
    live = (place * cols < width).astype(jnp.int32)

    half = rows // 2
    chunks = [slice(0, half), slice(half, rows)]
    sheets = [slice(0, half + 3), slice(half + 3, rows + 3)]
    chosen = []
    for at in sheets:
        for shift in range(nz):
            one = held[0][at]
            for k in range(1, ny):
                one = jnp.where(picks[shift] == k, held[k][at], one)
            chosen.append(one)
    chosen[:nz] = lax.optimization_barrier(tuple(chosen[:nz]))
    values = []
    for i in range(2):
        sent = chosen[i * nz : (i + 1) * nz]
        if i > 0:
            *sent, _ = lax.optimization_barrier((*sent, values[0]))
        values += [across(sent[shift], shift, ny, nz) for shift in range(nz)]
    taps = jnp.transpose(conv_weight, (0, 3, 1, 2)).reshape(3 * chans, 3 * chans)
    attended = [
        attend(
            live, query_weight, key_weight, taps, grad_out[at], sheet, at.start, values[: (i + 1) * nz]
        )
        for i, at in enumerate(chunks)
    ]
    refined = jnp.concatenate([done[0] for done in attended], axis=0)
    conv = jnp.concatenate([done[2] for done in attended], axis=0)

    first = lax.axis_index("eye") == 0
    sums = attended[0][7] + attended[1][7]
    total = jnp.where(first, sums[0], sums[1]) + swap_eyes(jnp.where(first, sums[1], sums[0]))
    riders = total.astype(jnp.bfloat16).reshape(-1, chans, cols)
    dfeats = []
    for i, done in enumerate(attended):
        dfeat = done[1]
        count = dfeat.shape[0]
        returned = []
        for shift in range(nz):
            block = done[3 + shift]
            if i == 1:
                block = jnp.concatenate([block, riders], axis=0)
            returned.append(across(block, -shift, ny, nz))
        if i == 1:
            total = sum_four(*[block[count:] for block in returned]).astype(jnp.bfloat16)
        lumps = []
        for k in range(ny):
            lump = jnp.zeros(dfeat.shape, jnp.float32)
            for shift in range(nz):
                part = returned[shift][:count].astype(jnp.float32)
                lump = lump + jnp.where(picks[shift] == k, part, 0.0)
            lumps.append(lump)
        moved = []
        for k in range(1, ny):
            lump = lumps[k].astype(jnp.bfloat16)
            if i == 1:
                lump = jnp.concatenate([lump, total], axis=0)
            moved.append(permute(lump, "y", -k, ny, nz))
        dfeat = dfeat + lumps[0]
        for lump in moved:
            dfeat = dfeat + lump[:count].astype(jnp.float32)
        if i == 1:
            total = sum_four(total, *[lump[count:] for lump in moved])
        dfeats.append(dfeat)
    total = total.reshape(-1, cols)
    dfeat = jnp.concatenate(dfeats, axis=0)
    dconv = (dfeat * jnp.where(conv > 0, 1.0, 0.1)).astype(jnp.bfloat16)
    n_row = lax.axis_size("row")
    row = lax.axis_index("row")
    own = total.astype(jnp.bfloat16)
    total = own.reshape(-1, chans, cols)
    up = lax.ppermute(
        jnp.concatenate([dconv[-1:], total]), "row", [(i, (i + 1) % n_row) for i in range(n_row)]
    )
    down = lax.ppermute(
        jnp.concatenate([dconv[:1], total]), "row", [(i, (i - 1) % n_row) for i in range(n_row)]
    )
    other = jnp.where(row % 2 == 0, down[1:], up[1:]).reshape(own.shape)
    total = own.astype(jnp.float32) + other.astype(jnp.float32)
    up = jnp.where(row == 0, 0.0, up[:1]).astype(jnp.bfloat16)
    down = jnp.where(row == n_row - 1, 0.0, down[:1]).astype(jnp.bfloat16)
    total, up, down = lax.optimization_barrier((total, up, down))
    tall = [up, dconv, down]
    left = shifted(jnp.concatenate([block[:, :, -1] for block in tall]), "col", 1)
    right = shifted(jnp.concatenate([block[:, :, 0] for block in tall]), "col", -1)
    step = 2
    while step < n_row:
        total = sum_pair(total, "row", step)
        step *= 2
    total, left, right = lax.optimization_barrier((total, left, right))
    edges = edge_tile(left, right, cols)
    turned = jnp.transpose(conv_weight[:, ::-1], (0, 2, 1, 3)).reshape(3 * chans, 3 * chans)
    input_grad = convolve_back(turned, dfeat, up, dconv, down, edges)
    conv_grad, query_grad, key_grad = join_eyes(total)
    return (refined[None], input_grad[None], conv_grad, query_grad, key_grad)


def solution(mesh):
    return jax.shard_map(
        body,
        mesh=mesh,
        in_specs=(
            P("eye", "row", None, "col"),
            P("eye", "row", None, "col"),
            P(),
            P(),
            P(),
            P("eye", "row", "col"),
            P("eye", "row", "col"),
        ),
        out_specs=(P("eye", "row", None, "col"), P("eye", "row", None, "col"), P(), P(), P()),
        check_vma=False,
    )
```

```python
import functools

import jax
import jax.numpy as jnp
from jax import lax
from jax.experimental import pallas as pl
from jax.experimental.pallas import tpu as pltpu
from jax.sharding import PartitionSpec as P

BAND_PANELS = 4
LOG2E = 1.4426950408889634


def shifted(block, axis, step):
    count = lax.axis_size(axis)
    moved = lax.ppermute(block, axis, [(i, (i + step) % count) for i in range(count)])
    edge = 0 if step > 0 else count - 1
    return jnp.where(lax.axis_index(axis) == edge, jnp.zeros_like(moved), moved)


def row_halo(block):
    up = shifted(block[-1:], "row", 1)
    down = shifted(block[:1], "row", -1)
    return jnp.concatenate([up, block, down], axis=0)


def edge_tile(left, right, cols):
    pad = ((0, 0), (0, cols // 2 - left.shape[0]))
    return jnp.concatenate([jnp.pad(left.T, pad), jnp.pad(right.T, pad)], axis=1)


def dot(lhs, rhs, dims):
    return lax.dot_general(lhs, rhs, (dims, ((), ())), preferred_element_type=jnp.float32)


NN = ((1,), (0,))
NT = ((1,), (1,))
TN = ((0,), (0,))


def with_columns(middle, edges, line):
    cols = middle.shape[1]
    lane = lax.broadcasted_iota(jnp.int32, middle.shape, 1)
    low = jnp.where(lane == 0, edges[:, line : line + 1], pltpu.roll(middle, 1, 1))
    at = cols // 2 + line
    high = jnp.where(lane == cols - 1, edges[:, at : at + 1], pltpu.roll(middle, cols - 1, 1))
    return jnp.concatenate([low, middle, high], axis=0).astype(jnp.bfloat16)


def back_kernel(taps_ref, dfeat_ref, up_ref, dconv_ref, down_ref, edge_ref, out_ref):
    rows, chans, cols = dfeat_ref.shape
    edges = edge_ref[...].astype(jnp.float32)
    tall = [up_ref[0]] + [dconv_ref[h] for h in range(rows)] + [down_ref[0]]
    wide = [with_columns(tall[r].astype(jnp.float32), edges, r) for r in range(rows + 2)]
    lines = dot(taps_ref[...], jnp.concatenate(wide, axis=1), NN)
    for h in range(rows):
        total = dfeat_ref[h]
        for a in range(3):
            at = (h + 2 - a) * cols
            total = total + lines[a * chans : (a + 1) * chans, at : at + cols]
        out_ref[h] = total.astype(jnp.bfloat16)


def convolve_back(taps, dfeat, up, dconv, down, edges):
    rows, chans, cols = dfeat.shape
    return pl.pallas_call(
        back_kernel,
        in_specs=[pl.BlockSpec(memory_space=pltpu.VMEM)] * 6,
        out_specs=pl.BlockSpec(memory_space=pltpu.VMEM),
        out_shape=jax.ShapeDtypeStruct(dfeat.shape, jnp.bfloat16),
        compiler_params=pltpu.CompilerParams(vmem_limit_bytes=16 * 1024 * 1024),
        cost_estimate=pl.CostEstimate(
            flops=2 * (rows + 2) * cols * 9 * chans * chans, bytes_accessed=10 * rows * chans * cols, transcendentals=0
        ),
    )(taps, dfeat, up, dconv, down, edges)


def attend_kernel(scale, first, rows, live_ref, wq_ref, wk_ref, wc_ref, grad_ref, own_ref, *refs):
    count = len(refs) - 8
    bands = [refs[o:count:BAND_PANELS] for o in range(BAND_PANELS)]
    refined_ref, part_ref, conv_ref, x0_ref, x1_ref, x2_ref, x3_ref, sums_ref = refs[count:]
    crosses = (x0_ref, x1_ref, x2_ref, x3_ref)
    chans, cols = own_ref.shape[1:]
    wq = wq_ref[...]
    wk = wk_ref[...]

    def image(source, skip, line):
        line = line - skip if line > 0 else 0
        for ref in source:
            if line < ref.shape[0]:
                return ref[line].astype(jnp.float32)
            line -= ref.shape[0]

    sources = [((own_ref,), 0)] + [(band, first) for band in bands]
    edges = [image(*source, 0) for source in sources]
    wide = [
        jnp.concatenate(
            [
                with_columns(image(*s, 1 + first + r), e, first + r)
                for s, e in zip(sources, edges)
            ],
            axis=1,
        )
        for r in range(rows + 2)
    ]
    lines = [dot(wc_ref[...], block, NN) for block in wide]
    convs = [
        lines[h][:chans] + lines[h + 1][chans : 2 * chans] + lines[h + 2][2 * chans :]
        for h in range(rows)
    ]
    feats = [
        (
            wide[h + 1][chans : 2 * chans].astype(jnp.float32)
            + jnp.where(convs[h] > 0, convs[h], 0.1 * convs[h])
        ).astype(jnp.bfloat16)
        for h in range(rows)
    ]
    feat_all = jnp.concatenate([feat[:, :cols] for feat in feats], axis=1)
    value_rows = [feat[:, cols:] for feat in feats]
    query_all = dot(wq.T, feat_all, NN).astype(jnp.bfloat16)
    keyed_all = dot(wk, query_all, NN) * scale
    keyed_b = keyed_all.astype(jnp.bfloat16)
    keyed_2 = (keyed_all * LOG2E).astype(jnp.bfloat16)
    spans = [slice(h * cols, (h + 1) * cols) for h in range(rows)]

    pairs = [
        dot(jnp.concatenate([keyed_2[:, spans[h]], grad_ref[h]], axis=1).T, value_rows[h], NN)
        for h in range(rows)
    ]
    probs = []
    for pair in pairs:
        score = jnp.concatenate(
            [
                jnp.where(live_ref[o] > 0, pair[:cols, o * cols : (o + 1) * cols], -jnp.inf)
                for o in range(BAND_PANELS)
            ],
            axis=1,
        )
        dprob = pair[cols:]
        expo = jnp.exp2(score - jnp.max(score, axis=1, keepdims=True))
        prob = expo * (1.0 / jnp.sum(expo, axis=1, keepdims=True))
        delta = jnp.sum(prob * dprob, axis=1, keepdims=True)
        dscore = prob * (dprob - delta)
        probs.append(
            jnp.concatenate([prob.astype(jnp.bfloat16), dscore.astype(jnp.bfloat16)], axis=0)
        )
    moved = []
    passed = []
    for h in range(rows):
        lhs = jnp.concatenate([grad_ref[h], keyed_b[:, spans[h]]], axis=1)
        cross = dot(lhs, probs[h], NN)
        passed.append(cross)
        for o in range(BAND_PANELS):
            crosses[o][h] = cross[:, o * cols : (o + 1) * cols].astype(jnp.bfloat16)
        summed = dot(value_rows[h], probs[h], NT)
        refined_ref[h] = (feats[h][:, :cols].astype(jnp.float32) + summed[:, :cols]).astype(
            jnp.bfloat16
        )
        moved.append((summed[:, cols:] * scale).astype(jnp.bfloat16))
    moved_all = jnp.concatenate(moved, axis=1)
    dquery = dot(wk.T, moved_all, NN).astype(jnp.bfloat16)
    part_all = dot(wq, dquery, NN)
    shares = []
    for h in range(rows):
        part = grad_ref[h].astype(jnp.float32) + part_all[:, spans[h]]
        part_ref[h] = part
        conv_ref[h] = convs[h][:, :cols]
        share = jnp.concatenate([part, passed[h]], axis=1)
        shares.append((share * jnp.where(convs[h] > 0, 1.0, 0.1)).astype(jnp.bfloat16))
    none = jnp.zeros_like(shares[0])
    total = jnp.zeros((3 * chans, 3 * chans), jnp.float32)
    for r in range(rows + 2):
        taps = [shares[r - a] if 0 <= r - a < rows else none for a in range(3)]
        total = total + dot(wide[r], jnp.concatenate(taps, axis=0), NT)
    sums_ref[0] = total[:, : 2 * chans]
    square = jnp.concatenate([dot(feat_all, dquery, NT), dot(moved_all, query_all, NT)], axis=0)
    square = jnp.concatenate([square, jnp.zeros((chans, chans), jnp.float32)], axis=0)
    sums_ref[1] = jnp.concatenate([total[:, 2 * chans :], square], axis=1)


def attend(live, wq, wk, wc, grad, own, first, values):
    rows, chans, cols = grad.shape
    whole = pl.BlockSpec(memory_space=pltpu.VMEM)
    tile_b = jax.ShapeDtypeStruct((rows, chans, cols), jnp.bfloat16)
    tile_f = jax.ShapeDtypeStruct((rows, chans, cols), jnp.float32)
    sums = jax.ShapeDtypeStruct((2, 3 * chans, 2 * chans), jnp.float32)
    flops = 2 * rows * chans * cols * cols * BAND_PANELS * 12
    return pl.pallas_call(
        functools.partial(attend_kernel, chans ** -0.5, first, rows),
        in_specs=[pl.BlockSpec(memory_space=pltpu.SMEM)] + [whole] * (5 + len(values)),
        out_specs=[whole] * 8,
        out_shape=[tile_b, tile_f, tile_f] + [tile_b] * 4 + [sums],
        compiler_params=pltpu.CompilerParams(vmem_limit_bytes=16 * 1024 * 1024),
        cost_estimate=pl.CostEstimate(
            flops=flops, bytes_accessed=20 * rows * chans * cols * 2, transcendentals=rows * cols * cols * 4
        ),
    )(live, wq, wk, wc, grad, own, *values)


def permute(block, axis, shift, ny, nz):
    if axis == "y":
        perm = [(y * nz + z, ((y + shift) % ny) * nz + z) for y in range(ny) for z in range(nz)]
    else:
        perm = [(y * nz + z, y * nz + (z + shift) % nz) for y in range(ny) for z in range(nz)]
    return lax.ppermute(block, "col", perm)


def across(block, shift, ny, nz):
    perm = [
        (e * ny * nz + y * nz + z, (1 - e) * ny * nz + y * nz + (z + shift) % nz)
        for e in range(2)
        for y in range(ny)
        for z in range(nz)
    ]
    return lax.ppermute(block, ("eye", "col"), perm)


def swap_eyes(block):
    return lax.ppermute(block, "eye", [(0, 1), (1, 0)])


def sum_pair(block, axis, step):
    block = block.astype(jnp.bfloat16)
    size = lax.axis_size(axis)
    perm = [(i, i // (2 * step) * 2 * step + (i + step) % (2 * step)) for i in range(size)]
    other = lax.ppermute(block, axis, perm)
    return block.astype(jnp.float32) + other.astype(jnp.float32)


def sum_four(own, near, far, last):
    own, near, far, last = [value.astype(jnp.float32) for value in (own, near, far, last)]
    return (own + far) + (near + last)


def join_eyes(total):
    chans = total.shape[1] // 2
    first = lax.axis_index("eye") == 0
    other = swap_eyes(total)
    lower, upper = jnp.where(first, other, total), jnp.where(first, total, other)
    taps = [lower[:, :chans], lower[:, chans:], upper[:, :chans]]
    conv_grad = jnp.stack([tap.reshape(3, chans, chans) for tap in taps])
    return conv_grad, upper[:chans, chans:], upper[chans : 2 * chans, chans:]


def body(images, cotangent, conv_weight, query_weight, key_weight, band_start, band_width):
    source = images[0]
    grad_out = cotangent[0]
    rows, chans, cols = source.shape
    nz = BAND_PANELS
    ny = lax.axis_size("col") // nz
    col = lax.axis_index("col")
    my_y = col // nz
    my_z = col % nz
    panel = band_start[0, 0, 0] // cols
    width = band_width[0, 0, 0]
    padded = lax.optimization_barrier(row_halo(source))
    left = shifted(padded[:, :, -1], "col", 1)
    right = shifted(padded[:, :, 0], "col", -1)
    sheet = jnp.concatenate([edge_tile(left, right, cols)[None], padded], axis=0)
    sheet, mark = lax.optimization_barrier((sheet, jnp.full((1, cols), panel)))
    held = [sheet] + [permute(sheet, "y", shift, ny, nz) for shift in range(1, ny)]
    known = [across(mark, -shift, ny, nz) for shift in range(nz)]
    picks = []
    for shift in range(nz):
        target = known[shift][0, 0]
        wanted = target + (my_z - target) % nz
        picks.append((my_y - wanted // nz) % ny)
    place = (my_z - jnp.arange(nz, dtype=jnp.int32) - panel) % nz
    live = (place * cols < width).astype(jnp.int32)

    half = rows // 2
    chunks = [slice(0, half), slice(half, rows)]
    sheets = [slice(0, half + 3), slice(half + 3, rows + 3)]
    chosen = []
    for at in sheets:
        for shift in range(nz):
            one = held[0][at]
            for k in range(1, ny):
                one = jnp.where(picks[shift] == k, held[k][at], one)
            chosen.append(one)
    chosen[:nz] = lax.optimization_barrier(tuple(chosen[:nz]))
    values = []
    for i in range(2):
        sent = chosen[i * nz : (i + 1) * nz]
        if i > 0:
            *sent, _ = lax.optimization_barrier((*sent, values[0]))
        values += [across(sent[shift], shift, ny, nz) for shift in range(nz)]
    taps = jnp.transpose(conv_weight, (0, 3, 1, 2)).reshape(3 * chans, 3 * chans)
    carried = [jnp.concatenate([one[:1], one[half + 1 :]]) for one in values[:nz]]
    bands = [values[:nz], carried + values[nz:]]
    attended = [
        attend(live, query_weight, key_weight, taps, grad_out[at], sheet, at.start, band)
        for at, band in zip(chunks, bands)
    ]
    refined = jnp.concatenate([done[0] for done in attended], axis=0)
    conv = jnp.concatenate([done[2] for done in attended], axis=0)

    first = lax.axis_index("eye") == 0
    sums = attended[0][7] + attended[1][7]
    early = [across(attended[0][3 + shift], -shift, ny, nz) for shift in range(nz)]
    sums, *early = lax.optimization_barrier((sums, *early))
    total = jnp.where(first, sums[0], sums[1]) + swap_eyes(jnp.where(first, sums[1], sums[0]))
    riders = total.astype(jnp.bfloat16).reshape(-1, chans, cols)
    dfeats = []
    for i, done in enumerate(attended):
        dfeat = done[1]
        count = dfeat.shape[0]
        returned = []
        for shift in range(nz):
            block = done[3 + shift]
            if i == 1:
                block = jnp.concatenate([block, riders], axis=0)
            returned.append(early[shift] if i == 0 else across(block, -shift, ny, nz))
        if i == 1:
            total = sum_four(*[block[count:] for block in returned]).astype(jnp.bfloat16)
        lumps = []
        for k in range(ny):
            lump = jnp.zeros(dfeat.shape, jnp.float32)
            for shift in range(nz):
                part = returned[shift][:count].astype(jnp.float32)
                lump = lump + jnp.where(picks[shift] == k, part, 0.0)
            lumps.append(lump)
        moved = []
        for k in range(1, ny):
            lump = lumps[k].astype(jnp.bfloat16)
            if i == 1:
                lump = jnp.concatenate([lump, total], axis=0)
            moved.append(permute(lump, "y", -k, ny, nz))
        dfeat = dfeat + lumps[0]
        for lump in moved:
            dfeat = dfeat + lump[:count].astype(jnp.float32)
        if i == 1:
            total = sum_four(total, *[lump[count:] for lump in moved])
        dfeats.append(dfeat)
    total = total.reshape(-1, cols)
    dfeat = jnp.concatenate(dfeats, axis=0)
    dconv = (dfeat * jnp.where(conv > 0, 1.0, 0.1)).astype(jnp.bfloat16)
    n_row = lax.axis_size("row")
    row = lax.axis_index("row")
    own = total.astype(jnp.bfloat16)
    total = own.reshape(-1, chans, cols)
    up = lax.ppermute(
        jnp.concatenate([dconv[-1:], total]), "row", [(i, (i + 1) % n_row) for i in range(n_row)]
    )
    down = lax.ppermute(
        jnp.concatenate([dconv[:1], total]), "row", [(i, (i - 1) % n_row) for i in range(n_row)]
    )
    other = jnp.where(row % 2 == 0, down[1:], up[1:]).reshape(own.shape)
    total = own.astype(jnp.float32) + other.astype(jnp.float32)
    up = jnp.where(row == 0, 0.0, up[:1]).astype(jnp.bfloat16)
    down = jnp.where(row == n_row - 1, 0.0, down[:1]).astype(jnp.bfloat16)
    total, up, down = lax.optimization_barrier((total, up, down))
    tall = [up, dconv, down]
    left = shifted(jnp.concatenate([block[:, :, -1] for block in tall]), "col", 1)
    right = shifted(jnp.concatenate([block[:, :, 0] for block in tall]), "col", -1)
    step = 2
    while step < n_row:
        total = sum_pair(total, "row", step)
        step *= 2
    total, left, right = lax.optimization_barrier((total, left, right))
    edges = edge_tile(left, right, cols)
    turned = jnp.transpose(conv_weight[:, ::-1], (0, 2, 1, 3)).reshape(3 * chans, 3 * chans)
    input_grad = convolve_back(turned, dfeat, up, dconv, down, edges)
    conv_grad, query_grad, key_grad = join_eyes(total)
    return (refined[None], input_grad[None], conv_grad, query_grad, key_grad)


def solution(mesh):
    return jax.shard_map(
        body,
        mesh=mesh,
        in_specs=(
            P("eye", "row", None, "col"),
            P("eye", "row", None, "col"),
            P(),
            P(),
            P(),
            P("eye", "row", "col"),
            P("eye", "row", "col"),
        ),
        out_specs=(P("eye", "row", None, "col"), P("eye", "row", None, "col"), P(), P(), P()),
        check_vma=False,
    )
```

```python
import functools

import jax
import jax.numpy as jnp
from jax import lax
from jax.experimental import pallas as pl
from jax.experimental.pallas import tpu as pltpu
from jax.sharding import PartitionSpec as P

BAND_PANELS = 4
LOG2E = 1.4426950408889634


def shifted(block, axis, step):
    count = lax.axis_size(axis)
    moved = lax.ppermute(block, axis, [(i, (i + step) % count) for i in range(count)])
    edge = 0 if step > 0 else count - 1
    return jnp.where(lax.axis_index(axis) == edge, jnp.zeros_like(moved), moved)


def row_halo(block):
    up = shifted(block[-1:], "row", 1)
    down = shifted(block[:1], "row", -1)
    return jnp.concatenate([up, block, down], axis=0)


def edge_tile(left, right, cols):
    pad = ((0, 0), (0, cols // 2 - left.shape[0]))
    return jnp.concatenate([jnp.pad(left.T, pad), jnp.pad(right.T, pad)], axis=1)


def dot(lhs, rhs, dims):
    return lax.dot_general(lhs, rhs, (dims, ((), ())), preferred_element_type=jnp.float32)


NN = ((1,), (0,))
NT = ((1,), (1,))
TN = ((0,), (0,))


def with_columns(middle, edges, line):
    cols = middle.shape[1]
    lane = lax.broadcasted_iota(jnp.int32, middle.shape, 1)
    low = jnp.where(lane == 0, edges[:, line : line + 1], pltpu.roll(middle, 1, 1))
    at = cols // 2 + line
    high = jnp.where(lane == cols - 1, edges[:, at : at + 1], pltpu.roll(middle, cols - 1, 1))
    return jnp.concatenate([low, middle, high], axis=0).astype(jnp.bfloat16)


def back_kernel(taps_ref, dfeat_ref, up_ref, dconv_ref, down_ref, edge_ref, out_ref):
    rows, chans, cols = dfeat_ref.shape
    edges = edge_ref[...].astype(jnp.float32)
    tall = [up_ref[0]] + [dconv_ref[h] for h in range(rows)] + [down_ref[0]]
    wide = [with_columns(tall[r].astype(jnp.float32), edges, r) for r in range(rows + 2)]
    lines = dot(taps_ref[...], jnp.concatenate(wide, axis=1), NN)
    for h in range(rows):
        total = dfeat_ref[h]
        for a in range(3):
            at = (h + 2 - a) * cols
            total = total + lines[a * chans : (a + 1) * chans, at : at + cols]
        out_ref[h] = total.astype(jnp.bfloat16)


def convolve_back(taps, dfeat, up, dconv, down, edges):
    rows, chans, cols = dfeat.shape
    return pl.pallas_call(
        back_kernel,
        in_specs=[pl.BlockSpec(memory_space=pltpu.VMEM)] * 6,
        out_specs=pl.BlockSpec(memory_space=pltpu.VMEM),
        out_shape=jax.ShapeDtypeStruct(dfeat.shape, jnp.bfloat16),
        compiler_params=pltpu.CompilerParams(vmem_limit_bytes=16 * 1024 * 1024),
        cost_estimate=pl.CostEstimate(
            flops=2 * (rows + 2) * cols * 9 * chans * chans, bytes_accessed=10 * rows * chans * cols, transcendentals=0
        ),
    )(taps, dfeat, up, dconv, down, edges)


def attend_kernel(scale, first, rows, live_ref, wq_ref, wk_ref, wc_ref, grad_ref, own_ref, *refs):
    count = len(refs) - 8
    bands = [refs[o:count:BAND_PANELS] for o in range(BAND_PANELS)]
    refined_ref, part_ref, conv_ref, x0_ref, x1_ref, x2_ref, x3_ref, sums_ref = refs[count:]
    crosses = (x0_ref, x1_ref, x2_ref, x3_ref)
    chans, cols = own_ref.shape[1:]
    wq = wq_ref[...]
    wk = wk_ref[...]

    def image(source, skip, line):
        line = line - skip if line > 0 else 0
        for ref in source:
            if line < ref.shape[0]:
                return ref[line].astype(jnp.float32)
            line -= ref.shape[0]

    sources = [((own_ref,), 0)] + [(band, first) for band in bands]
    edges = [image(*source, 0) for source in sources]
    wide = [
        jnp.concatenate(
            [
                with_columns(image(*s, 1 + first + r), e, first + r)
                for s, e in zip(sources, edges)
            ],
            axis=1,
        )
        for r in range(rows + 2)
    ]
    lines = [dot(wc_ref[...], block, NN) for block in wide]
    convs = [
        lines[h][:chans] + lines[h + 1][chans : 2 * chans] + lines[h + 2][2 * chans :]
        for h in range(rows)
    ]
    feats = [
        (
            wide[h + 1][chans : 2 * chans].astype(jnp.float32)
            + jnp.where(convs[h] > 0, convs[h], 0.1 * convs[h])
        ).astype(jnp.bfloat16)
        for h in range(rows)
    ]
    feat_all = jnp.concatenate([feat[:, :cols] for feat in feats], axis=1)
    value_rows = [feat[:, cols:] for feat in feats]
    query_all = dot(wq.T, feat_all, NN).astype(jnp.bfloat16)
    keyed_all = dot(wk, query_all, NN) * scale
    keyed_b = keyed_all.astype(jnp.bfloat16)
    keyed_2 = (keyed_all * LOG2E).astype(jnp.bfloat16)
    spans = [slice(h * cols, (h + 1) * cols) for h in range(rows)]

    pairs = [
        dot(jnp.concatenate([keyed_2[:, spans[h]], grad_ref[h]], axis=1).T, value_rows[h], NN)
        for h in range(rows)
    ]
    probs = []
    for pair in pairs:
        score = jnp.concatenate(
            [
                jnp.where(live_ref[o] > 0, pair[:cols, o * cols : (o + 1) * cols], -jnp.inf)
                for o in range(BAND_PANELS)
            ],
            axis=1,
        )
        dprob = pair[cols:]
        expo = jnp.exp2(score - jnp.max(score, axis=1, keepdims=True))
        prob = expo * (1.0 / jnp.sum(expo, axis=1, keepdims=True))
        delta = jnp.sum(prob * dprob, axis=1, keepdims=True)
        dscore = prob * (dprob - delta)
        probs.append(
            jnp.concatenate([prob.astype(jnp.bfloat16), dscore.astype(jnp.bfloat16)], axis=0)
        )
    moved = []
    passed = []
    for h in range(rows):
        lhs = jnp.concatenate([grad_ref[h], keyed_b[:, spans[h]]], axis=1)
        cross = dot(lhs, probs[h], NN)
        passed.append(cross)
        for o in range(BAND_PANELS):
            crosses[o][h] = cross[:, o * cols : (o + 1) * cols].astype(jnp.bfloat16)
        summed = dot(value_rows[h], probs[h], NT)
        refined_ref[h] = (feats[h][:, :cols].astype(jnp.float32) + summed[:, :cols]).astype(
            jnp.bfloat16
        )
        moved.append((summed[:, cols:] * scale).astype(jnp.bfloat16))
    moved_all = jnp.concatenate(moved, axis=1)
    dquery = dot(wk.T, moved_all, NN).astype(jnp.bfloat16)
    part_all = dot(wq, dquery, NN)
    shares = []
    for h in range(rows):
        part = grad_ref[h].astype(jnp.float32) + part_all[:, spans[h]]
        part_ref[h] = part
        conv_ref[h] = convs[h][:, :cols]
        share = jnp.concatenate([part, passed[h]], axis=1)
        shares.append((share * jnp.where(convs[h] > 0, 1.0, 0.1)).astype(jnp.bfloat16))
    none = jnp.zeros_like(shares[0])
    total = jnp.zeros((3 * chans, 3 * chans), jnp.float32)
    for r in range(rows + 2):
        taps = [shares[r - a] if 0 <= r - a < rows else none for a in range(3)]
        total = total + dot(wide[r], jnp.concatenate(taps, axis=0), NT)
    sums_ref[0] = total[:, : 2 * chans]
    square = jnp.concatenate([dot(feat_all, dquery, NT), dot(moved_all, query_all, NT)], axis=0)
    square = jnp.concatenate([square, jnp.zeros((chans, chans), jnp.float32)], axis=0)
    sums_ref[1] = jnp.concatenate([total[:, 2 * chans :], square], axis=1)


def attend(live, wq, wk, wc, grad, own, first, values):
    rows, chans, cols = grad.shape
    whole = pl.BlockSpec(memory_space=pltpu.VMEM)
    tile_b = jax.ShapeDtypeStruct((rows, chans, cols), jnp.bfloat16)
    tile_f = jax.ShapeDtypeStruct((rows, chans, cols), jnp.float32)
    sums = jax.ShapeDtypeStruct((2, 3 * chans, 2 * chans), jnp.float32)
    flops = 2 * rows * chans * cols * cols * BAND_PANELS * 12
    return pl.pallas_call(
        functools.partial(attend_kernel, chans ** -0.5, first, rows),
        in_specs=[pl.BlockSpec(memory_space=pltpu.SMEM)] + [whole] * (5 + len(values)),
        out_specs=[whole] * 8,
        out_shape=[tile_b, tile_f, tile_f] + [tile_b] * 4 + [sums],
        compiler_params=pltpu.CompilerParams(vmem_limit_bytes=16 * 1024 * 1024),
        cost_estimate=pl.CostEstimate(
            flops=flops, bytes_accessed=20 * rows * chans * cols * 2, transcendentals=rows * cols * cols * 4
        ),
    )(live, wq, wk, wc, grad, own, *values)


def permute(block, axis, shift, ny, nz):
    if axis == "y":
        perm = [(y * nz + z, ((y + shift) % ny) * nz + z) for y in range(ny) for z in range(nz)]
    else:
        perm = [(y * nz + z, y * nz + (z + shift) % nz) for y in range(ny) for z in range(nz)]
    return lax.ppermute(block, "col", perm)


def across(block, shift, ny, nz):
    perm = [
        (e * ny * nz + y * nz + z, (1 - e) * ny * nz + y * nz + (z + shift) % nz)
        for e in range(2)
        for y in range(ny)
        for z in range(nz)
    ]
    return lax.ppermute(block, ("eye", "col"), perm)


def swap_eyes(block):
    return lax.ppermute(block, "eye", [(0, 1), (1, 0)])


def sum_pair(block, axis, step):
    block = block.astype(jnp.bfloat16)
    size = lax.axis_size(axis)
    perm = [(i, i // (2 * step) * 2 * step + (i + step) % (2 * step)) for i in range(size)]
    other = lax.ppermute(block, axis, perm)
    return block.astype(jnp.float32) + other.astype(jnp.float32)


def sum_four(own, near, far, last):
    own, near, far, last = [value.astype(jnp.float32) for value in (own, near, far, last)]
    return (own + far) + (near + last)


def join_eyes(total):
    chans = total.shape[1] // 2
    first = lax.axis_index("eye") == 0
    other = swap_eyes(total)
    lower, upper = jnp.where(first, other, total), jnp.where(first, total, other)
    taps = [lower[:, :chans], lower[:, chans:], upper[:, :chans]]
    conv_grad = jnp.stack([tap.reshape(3, chans, chans) for tap in taps])
    return conv_grad, upper[:chans, chans:], upper[chans : 2 * chans, chans:]


def body(images, cotangent, conv_weight, query_weight, key_weight, band_start, band_width):
    source = images[0]
    grad_out = cotangent[0]
    rows, chans, cols = source.shape
    nz = BAND_PANELS
    ny = lax.axis_size("col") // nz
    col = lax.axis_index("col")
    my_y = col // nz
    my_z = col % nz
    panel = band_start[0, 0, 0] // cols
    width = band_width[0, 0, 0]
    padded = lax.optimization_barrier(row_halo(source))
    left = shifted(padded[:, :, -1], "col", 1)
    right = shifted(padded[:, :, 0], "col", -1)
    sheet = jnp.concatenate([edge_tile(left, right, cols)[None], padded], axis=0)
    sheet, mark = lax.optimization_barrier((sheet, jnp.full((1, cols), panel)))
    held = [sheet] + [permute(sheet, "y", shift, ny, nz) for shift in range(1, ny)]
    known = [across(mark, -shift, ny, nz) for shift in range(nz)]
    picks = []
    for shift in range(nz):
        target = known[shift][0, 0]
        wanted = target + (my_z - target) % nz
        picks.append((my_y - wanted // nz) % ny)
    place = (my_z - jnp.arange(nz, dtype=jnp.int32) - panel) % nz
    live = (place * cols < width).astype(jnp.int32)

    half = rows // 2
    chunks = [slice(0, half), slice(half, rows)]
    sheets = [slice(0, half + 3), slice(half + 3, rows + 3)]
    chosen = []
    for at in sheets:
        for shift in range(nz):
            one = held[0][at]
            for k in range(1, ny):
                one = jnp.where(picks[shift] == k, held[k][at], one)
            chosen.append(one)
    chosen[:nz] = lax.optimization_barrier(tuple(chosen[:nz]))
    values = []
    for i in range(2):
        sent = chosen[i * nz : (i + 1) * nz]
        if i > 0:
            *sent, _ = lax.optimization_barrier((*sent, values[0]))
        values += [across(sent[shift], shift, ny, nz) for shift in range(nz)]
    taps = jnp.transpose(conv_weight, (0, 3, 1, 2)).reshape(3 * chans, 3 * chans)
    carried = [jnp.concatenate([one[:1], one[half + 1 :]]) for one in values[:nz]]
    bands = [values[:nz], carried + values[nz:]]
    attended = [
        attend(live, query_weight, key_weight, taps, grad_out[at], sheet, at.start, band)
        for at, band in zip(chunks, bands)
    ]
    refined = jnp.concatenate([done[0] for done in attended], axis=0)
    conv = jnp.concatenate([done[2] for done in attended], axis=0)

    first = lax.axis_index("eye") == 0
    sums = attended[0][7] + attended[1][7]
    early = [across(attended[0][3 + shift], -shift, ny, nz) for shift in range(nz)]
    sums, *early = lax.optimization_barrier((sums, *early))
    total = jnp.where(first, sums[0], sums[1]) + swap_eyes(jnp.where(first, sums[1], sums[0]))
    riders = total.astype(jnp.bfloat16).reshape(-1, chans, cols)
    dfeats = []
    for i, done in enumerate(attended):
        dfeat = done[1]
        count = dfeat.shape[0]
        returned = []
        for shift in range(nz):
            block = done[3 + shift]
            if i == 1:
                block = jnp.concatenate([block, riders], axis=0)
            returned.append(early[shift] if i == 0 else across(block, -shift, ny, nz))
        if i == 1:
            total = sum_four(*[block[count:] for block in returned]).astype(jnp.bfloat16)
        lumps = []
        for k in range(ny):
            lump = jnp.zeros(dfeat.shape, jnp.float32)
            for shift in range(nz):
                part = returned[shift][:count].astype(jnp.float32)
                lump = lump + jnp.where(picks[shift] == k, part, 0.0)
            lumps.append(lump)
        moved = []
        for k in range(1, ny):
            lump = lumps[k].astype(jnp.bfloat16)
            if i == 1:
                lump = jnp.concatenate([lump, total], axis=0)
            moved.append(permute(lump, "y", -k, ny, nz))
        dfeat = dfeat + lumps[0]
        for lump in moved:
            dfeat = dfeat + lump[:count].astype(jnp.float32)
        if i == 1:
            total = sum_four(total, *[lump[count:] for lump in moved])
        dfeats.append(dfeat)
    total = total.reshape(-1, cols)
    dfeat = jnp.concatenate(dfeats, axis=0)
    dconv = (dfeat * jnp.where(conv > 0, 1.0, 0.1)).astype(jnp.bfloat16)
    n_row = lax.axis_size("row")
    row = lax.axis_index("row")
    own = total.astype(jnp.bfloat16)
    total = own.reshape(-1, chans, cols)
    up = lax.ppermute(
        jnp.concatenate([dconv[-1:], total]), "row", [(i, (i + 1) % n_row) for i in range(n_row)]
    )
    down = lax.ppermute(
        jnp.concatenate([dconv[:1], total]), "row", [(i, (i - 1) % n_row) for i in range(n_row)]
    )
    other = jnp.where(row % 2 == 0, down[1:], up[1:]).reshape(own.shape)
    total = own.astype(jnp.float32) + other.astype(jnp.float32)
    up = jnp.where(row == 0, 0.0, up[:1]).astype(jnp.bfloat16)
    down = jnp.where(row == n_row - 1, 0.0, down[:1]).astype(jnp.bfloat16)
    total, up, down = lax.optimization_barrier((total, up, down))
    tall = [up, dconv, down]
    left = shifted(jnp.concatenate([block[:, :, -1] for block in tall]), "col", 1)
    right = shifted(jnp.concatenate([block[:, :, 0] for block in tall]), "col", -1)
    step = 2
    while step < n_row:
        total = sum_pair(total, "row", step)
        step *= 2
    total, left, right = lax.optimization_barrier((total, left, right))
    edges = edge_tile(left, right, cols)
    turned = jnp.transpose(conv_weight[:, ::-1], (0, 2, 1, 3)).reshape(3 * chans, 3 * chans)
    input_grad = convolve_back(turned, dfeat, up, dconv, down, edges)
    total, input_grad = lax.optimization_barrier((total, input_grad))
    conv_grad, query_grad, key_grad = join_eyes(total)
    return (refined[None], input_grad[None], conv_grad, query_grad, key_grad)


def solution(mesh):
    return jax.shard_map(
        body,
        mesh=mesh,
        in_specs=(
            P("eye", "row", None, "col"),
            P("eye", "row", None, "col"),
            P(),
            P(),
            P(),
            P("eye", "row", "col"),
            P("eye", "row", "col"),
        ),
        out_specs=(P("eye", "row", None, "col"), P("eye", "row", None, "col"), P(), P(), P()),
        check_vma=False,
    )
```
